32 devices in a mesh: head: 4 (over x, core), ctx: 8 (over z, y).
Axes of the slice: x: 2, y: 2, z: 4, core: 2. Of those that a mesh axis runs over, the one named last changes fastest.
Arguments:
- queries: bfloat16 [16, 4096, 128], P(None, ('ctx', 'head')), may hold values from -6 to 6
- key_rows: bfloat16 [4096, 128], P(('ctx', 'head')), may hold values from -6 to 6
- value_rows: bfloat16 [4096, 128], P(('ctx', 'head')), may hold values from -6 to 6
- attn_output: bfloat16 [16, 4096, 128], P(None, ('ctx', 'head')), may hold values from -6 to 6
- grad_output: bfloat16 [16, 4096, 128], P(None, ('ctx', 'head')), may hold values from -6 to 6
- logsumexp: float32 [16, 4096], P(None, ('ctx', 'head')), as said below
- positions: int32 [4096], P(('ctx', 'head')), may hold values from 0 to 4095, as said below
Outputs:
- grad_queries: bfloat16 [16, 4096, 128], P(None, ('ctx', 'head'))
- grad_keys: bfloat16 [4096, 128], P(('ctx', 'head'))
- grad_values: bfloat16 [4096, 128], P(('ctx', 'head'))
The draws below stay inside these ranges and needn't reach their ends.
Inputs may be any that keep to these rules, and one draw needn't show every extreme that they name: positions is a permutation of 0 to 4095. The sequence is cut into 16 runs of 256 consecutive positions; the 512 tokens of each index of ctx are, in order, one run r and then run 2 * 8 - 1 - r, each in increasing order; which r falls on which index is drawn. logsumexp[h, i] lies between log(positions[i] + 1) + 0.2 and log(positions[i] + 1) + 1.2.
All inputs are finite; a program needn't handle non-finite values.
Results may differ from the reference program's by a relative error of at most 0.0055.
Values may be sent and summed in bfloat16 or wider, within the bound.
A program may use at most 64 MiB of HBM per device.

```python
import math
import jax
import jax.numpy as jnp
from jax import lax

HEADS = 16
DH = 128
HALF = 256
PAIRS = 8
TOKENS = 4096


def run_positions(key):
    order = jax.random.permutation(key, PAIRS).astype(jnp.int32)
    offsets = jnp.arange(HALF, dtype=jnp.int32)
    early = order[:, None] * HALF + offsets[None, :]
    later = (2 * PAIRS - 1 - order)[:, None] * HALF + offsets[None, :]
    return jnp.concatenate([early, later], axis=1).reshape(TOKENS).astype(jnp.int32)


def draw_positions(key, part):
    return run_positions(key)


def draw_logsumexp(key, part):
    places = run_positions(key)
    key = jax.random.fold_in(key, 11)
    noise = jax.random.uniform(key, (HEADS, TOKENS), jnp.float32, 0.2, 1.2)
    return jnp.log(places.astype(jnp.float32) + 1.0)[None, :] + noise


def levels(key, shape, pieces, low, high):
    gain = 1.0
    for position, parts in pieces:
        draws = jax.random.uniform(jax.random.fold_in(jax.random.fold_in(key, 6), position), (parts,), jnp.float32, low / len(pieces), high / len(pieces))
        gain = gain * jnp.repeat(jnp.exp(draws), shape[position] // parts).reshape((-1,) + (1,) * (len(shape) - 1 - position))
    return gain


def centred(own_key, shape, spread, most, shards=(), kind=jnp.bfloat16):
    values = spread * jax.random.normal(own_key, shape, jnp.float32)
    if shards:
        values = values * levels(own_key, shape, shards, -0.22, 0.18)
    return jnp.clip(values, -most, most).astype(kind)


def setup_inputs(seed: int = 0) -> dict:
    key_of = jax.random.split(jax.random.key(seed), 8)
    queries = centred(key_of[0], (HEADS, TOKENS, DH), 1.0, 6.0, ((1, 32),))
    key_rows = centred(key_of[1], (TOKENS, DH), 1.0, 6.0, ((0, 32),))
    value_rows = centred(key_of[2], (TOKENS, DH), 1.0, 6.0, ((0, 32),))
    attn_output = centred(key_of[3], (HEADS, TOKENS, DH), 1.0, 6.0, ((1, 32),))
    grad_output = centred(key_of[4], (HEADS, TOKENS, DH), 1.0, 6.0, ((1, 32),))
    logsumexp = draw_logsumexp(jax.random.fold_in(key_of[7], 71), 0)
    positions = draw_positions(jax.random.fold_in(key_of[7], 71), 0)
    return {"queries": queries, "key_rows": key_rows, "value_rows": value_rows, "attn_output": attn_output, "grad_output": grad_output, "logsumexp": logsumexp, "positions": positions}


def reference(queries, key_rows, value_rows, attn_output, grad_output, logsumexp, positions):
    scaling = DH ** -0.5
    block_size = math.gcd(TOKENS, 128)
    blocks = TOKENS // block_size
    row_delta = jnp.sum(grad_output.astype(jnp.float32) * attn_output.astype(jnp.float32), axis=2)
    key_wide = key_rows.astype(jnp.float32)
    value_wide = value_rows.astype(jnp.float32)

    def one_block(carried, number):
        key_sum, value_sum = carried
        first_row = (number * block_size).astype(jnp.int32)
        query_part = lax.dynamic_slice_in_dim(queries, first_row, block_size, 1).astype(jnp.float32)
        grad_part = lax.dynamic_slice_in_dim(grad_output, first_row, block_size, 1).astype(jnp.float32)
        lse_part = lax.dynamic_slice_in_dim(logsumexp, first_row, block_size, 1)
        delta_part = lax.dynamic_slice_in_dim(row_delta, first_row, block_size, 1)
        place_part = lax.dynamic_slice_in_dim(positions, first_row, block_size, 0)
        scores = jnp.einsum("hqd,kd->hqk", query_part, key_wide) * scaling
        visible = positions[None, None, :] <= place_part[None, :, None]
        attention = jnp.where(visible, jnp.exp(scores - lse_part[:, :, None]), 0.0)
        attention_low = lax.optimization_barrier(attention.astype(jnp.bfloat16)).astype(jnp.float32)
        grad_probs = jnp.einsum("hqd,kd->hqk", grad_part, value_wide)
        grad_scores = attention * (grad_probs - delta_part[:, :, None])
        grad_scores = lax.optimization_barrier(grad_scores.astype(jnp.bfloat16)).astype(jnp.float32)
        query_grad = (jnp.einsum("hqk,kd->hqd", grad_scores, key_wide) * scaling).astype(jnp.bfloat16)
        key_sum = key_sum + jnp.einsum("hqk,hqd->kd", grad_scores, query_part)
        value_sum = value_sum + jnp.einsum("hqk,hqd->kd", attention_low, grad_part)
        return (key_sum, value_sum), query_grad

    start = (jnp.zeros((TOKENS, DH), jnp.float32), jnp.zeros((TOKENS, DH), jnp.float32))
    (key_sum, value_sum), query_blocks = lax.scan(one_block, start, jnp.arange(blocks, dtype=jnp.int32))
    grad_queries = query_blocks.transpose(1, 0, 2, 3).reshape(HEADS, TOKENS, DH)
    return grad_queries, (key_sum * scaling).astype(jnp.bfloat16), value_sum.astype(jnp.bfloat16)
```

```python
import functools
import math

import jax
import jax.numpy as jnp
from jax import lax
from jax.experimental import pallas as pl
from jax.experimental.pallas import tpu as pltpu
from jax.sharding import PartitionSpec as P


def contract(a, b, axes):
    return lax.dot_general(a, b, (axes, ((), ())), preferred_element_type=jnp.float32)


def tiles_kernel(cycle, runs_ref, mine_ref, qd_ref, lse_ref, delta_ref, kv_ref, dq_ref, dkv_ref, acc):
    heads, rows, wide = qd_ref.shape
    width = wide // 2
    run = rows // 2
    scaling = width ** (-0.5)
    log2e = 1.0 / math.log(2.0)
    me = mine_ref[0]
    my_run = runs_ref[me]
    acc[...] = jnp.zeros_like(acc)

    def unit(query_half, key_row, diagonal):
        rows_of = pl.ds(pl.multiple_of(query_half * run, run), run)
        keys_of = pl.ds(pl.multiple_of(key_row, run), run)
        query = qd_ref[:, rows_of, :width].reshape(heads * run, width)
        grad = qd_ref[:, rows_of, width:].reshape(heads * run, width)
        key = kv_ref[keys_of, :width]
        value = kv_ref[keys_of, width:]
        scores = contract(key, query, ((1,), (1,)))
        prob = jnp.exp2(scores * (scaling * log2e) - lse_ref[query_half] * log2e)
        if diagonal:
            key_at = lax.broadcasted_iota(jnp.int32, scores.shape, 0)
            query_at = lax.broadcasted_iota(jnp.int32, scores.shape, 1) % run
            prob = jnp.where(key_at <= query_at, prob, 0.0)
        grad_prob = contract(value, grad, ((1,), (1,)))
        grad_score = (prob * (grad_prob - delta_ref[query_half])).astype(jnp.bfloat16)
        value_grad = contract(prob.astype(jnp.bfloat16), grad, ((1,), (0,)))
        key_grad = contract(grad_score, query, ((1,), (0,)))
        acc[query_half] += contract(key.T, grad_score, ((1,), (0,)))
        return keys_of, key_grad * scaling, value_grad

    def put(terms):
        keys_of, key_grad, value_grad = terms
        dkv_ref[keys_of, :width] = key_grad
        dkv_ref[keys_of, width:] = value_grad

    def add(terms):
        keys_of, key_grad, value_grad = terms
        dkv_ref[keys_of, :width] += key_grad
        dkv_ref[keys_of, width:] += value_grad

    put(unit(1, me * rows, False))
    add(unit(0, me * rows, True))
    put(unit(1, me * rows + run, True))

    @pl.loop(1, cycle)
    def _(step):
        other = lax.rem(me + step, cycle)
        first = other * rows
        late = (runs_ref[other] > my_run).astype(jnp.int32)
        put(unit(1, first, False))
        dkv_ref[pl.ds(pl.multiple_of(first + run, run), run), :] = jnp.zeros((run, wide), jnp.float32)
        add(unit(late, first + late * run, False))

    for half in range(2):
        for head in range(heads):
            part = acc[half, :, head * run : (head + 1) * run] * scaling
            dq_ref[head, half * run : (half + 1) * run, :] = part.T.astype(jnp.bfloat16)


def tiles(cycle, runs, mine, qd, lse, delta, kv):
    heads, rows, wide = qd.shape
    whole = pl.BlockSpec(memory_space=pltpu.VMEM)
    scalars = pl.BlockSpec(memory_space=pltpu.SMEM)
    return pl.pallas_call(
        functools.partial(tiles_kernel, cycle),
        out_shape=(
            jax.ShapeDtypeStruct((heads, rows, wide // 2), jnp.bfloat16),
            jax.ShapeDtypeStruct(kv.shape, jnp.float32),
        ),
        in_specs=[scalars, scalars, whole, whole, whole, whole],
        out_specs=(whole, whole),
        scratch_shapes=[pltpu.VMEM((2, wide // 2, heads * rows // 2), jnp.float32)],
        compiler_params=pltpu.CompilerParams(vmem_limit_bytes=60 * 1024 * 1024),
    )(runs, mine, qd, lse, delta, kv)


def local(queries, key_rows, value_rows, attn_output, grad_output, logsumexp, positions):
    cycle = lax.axis_size("ctx")
    group = lax.axis_size("head")
    width = queries.shape[2]
    rows = positions.shape[0] * group
    run = rows // 2
    heads = queries.shape[0] // group
    row_delta = jnp.sum(grad_output.astype(jnp.float32) * attn_output.astype(jnp.float32), axis=2)
    kv = lax.all_gather(
        jnp.concatenate([key_rows, value_rows], axis=1), ("ctx", "head"), axis=0, tiled=True
    )
    places = lax.all_gather(positions, ("ctx", "head"), axis=0, tiled=True)
    runs = places.reshape(cycle, rows)[:, 0] // run
    mine = lax.axis_index("ctx").reshape(1)
    qd = lax.all_to_all(
        jnp.concatenate([queries, grad_output], axis=2), "head", split_axis=0, concat_axis=1, tiled=True
    )
    stats = lax.all_to_all(
        jnp.stack([logsumexp, row_delta], axis=1), "head", split_axis=0, concat_axis=2, tiled=True
    )
    stats = stats.reshape(heads, 2, 2, run).transpose(1, 2, 0, 3).reshape(2, 2, 1, heads * run)
    dq, dkv = tiles(cycle, runs, mine, qd, stats[0], stats[1], kv)
    mine_kv = lax.psum_scatter(dkv, ("ctx", "head"), scatter_dimension=0, tiled=True)
    grad_queries = lax.all_to_all(dq, "head", split_axis=1, concat_axis=0, tiled=True)
    return (
        grad_queries,
        mine_kv[:, :width].astype(jnp.bfloat16),
        mine_kv[:, width:].astype(jnp.bfloat16),
    )


def solution(mesh):
    return jax.shard_map(
        local,
        mesh=mesh,
        in_specs=(
            P(None, ("ctx", "head"), None),
            P(("ctx", "head"), None),
            P(("ctx", "head"), None),
            P(None, ("ctx", "head"), None),
            P(None, ("ctx", "head"), None),
            P(None, ("ctx", "head")),
            P(("ctx", "head")),
        ),
        out_specs=(
            P(None, ("ctx", "head"), None),
            P(("ctx", "head"), None),
            P(("ctx", "head"), None),
        ),
        check_vma=False,
    )
```

```python
import functools
import math

import jax
import jax.numpy as jnp
from jax import lax
from jax.experimental import pallas as pl
from jax.experimental.pallas import tpu as pltpu
from jax.sharding import PartitionSpec as P


def contract(a, b, axes):
    return lax.dot_general(a, b, (axes, ((), ())), preferred_element_type=jnp.float32)


def tiles_kernel(cycle, runs_ref, mine_ref, qd_ref, lse_ref, delta_ref, kv_ref, dq_ref, dkv_ref, acc):
    heads, rows, wide = qd_ref.shape
    width = wide // 2
    run = rows // 2
    scaling = width ** (-0.5)
    log2e = 1.0 / math.log(2.0)
    me = mine_ref[0]
    my_run = runs_ref[me]
    acc[...] = jnp.zeros_like(acc)

    def unit(query_half, key_row, diagonal):
        rows_of = pl.ds(pl.multiple_of(query_half * run, run), run)
        keys_of = pl.ds(pl.multiple_of(key_row, run), run)
        query = qd_ref[:, rows_of, :width].reshape(heads * run, width)
        grad = qd_ref[:, rows_of, width:].reshape(heads * run, width)
        key = kv_ref[keys_of, :width]
        value = kv_ref[keys_of, width:]
        scores = contract(key, query, ((1,), (1,)))
        prob = jnp.exp2(scores * (scaling * log2e) - lse_ref[query_half] * log2e)
        if diagonal:
            key_at = lax.broadcasted_iota(jnp.int32, scores.shape, 0)
            query_at = lax.broadcasted_iota(jnp.int32, scores.shape, 1) % run
            prob = jnp.where(key_at <= query_at, prob, 0.0)
        grad_prob = contract(value, grad, ((1,), (1,)))
        grad_score = (prob * (grad_prob - delta_ref[query_half])).astype(jnp.bfloat16)
        value_grad = contract(prob.astype(jnp.bfloat16), grad, ((1,), (0,)))
        key_grad = contract(grad_score, query, ((1,), (0,)))
        acc[query_half] += contract(key.T, grad_score, ((1,), (0,)))
        return keys_of, key_grad * scaling, value_grad

    def put(terms):
        keys_of, key_grad, value_grad = terms
        dkv_ref[keys_of, :width] = key_grad
        dkv_ref[keys_of, width:] = value_grad

    def add(terms):
        keys_of, key_grad, value_grad = terms
        dkv_ref[keys_of, :width] += key_grad
        dkv_ref[keys_of, width:] += value_grad

    put(unit(1, me * rows, False))
    add(unit(0, me * rows, True))
    put(unit(1, me * rows + run, True))

    @pl.loop(1, cycle)
    def _(step):
        other = lax.rem(me + step, cycle)
        first = other * rows
        late = (runs_ref[other] > my_run).astype(jnp.int32)
        put(unit(1, first, False))
        dkv_ref[pl.ds(pl.multiple_of(first + run, run), run), :] = jnp.zeros((run, wide), jnp.float32)
        add(unit(late, first + late * run, False))

    for half in range(2):
        for head in range(heads):
            part = acc[half, :, head * run : (head + 1) * run] * scaling
            dq_ref[head, half * run : (half + 1) * run, :] = part.T.astype(jnp.bfloat16)


def tiles(cycle, runs, mine, qd, lse, delta, kv):
    heads, rows, wide = qd.shape
    whole = pl.BlockSpec(memory_space=pltpu.VMEM)
    scalars = pl.BlockSpec(memory_space=pltpu.SMEM)
    return pl.pallas_call(
        functools.partial(tiles_kernel, cycle),
        out_shape=(
            jax.ShapeDtypeStruct((heads, rows, wide // 2), jnp.bfloat16),
            jax.ShapeDtypeStruct(kv.shape, jnp.float32),
        ),
        in_specs=[scalars, scalars, whole, whole, whole, whole],
        out_specs=(whole, whole),
        scratch_shapes=[pltpu.VMEM((2, wide // 2, heads * rows // 2), jnp.float32)],
        compiler_params=pltpu.CompilerParams(vmem_limit_bytes=60 * 1024 * 1024),
    )(runs, mine, qd, lse, delta, kv)


MESH = pl.DeviceIdType.MESH


def digits_of(cycle):
    return {8: (4, 2), 32: (4, 4, 2)}.get(cycle, (cycle,))


def split_index(index, digits):
    parts = []
    for size in reversed(digits):
        parts.append(lax.rem(index, size))
        index = lax.div(index, size)
    return parts[::-1]


def join_index(parts, digits):
    index = 0
    for part, size in zip(parts, digits):
        index = index * size + part
    return index


def greet(peers):
    barrier = pltpu.get_barrier_semaphore()
    for head, ctx in peers:
        pl.semaphore_signal(barrier, inc=1, device_id=(head, ctx), device_id_type=MESH)
    pl.semaphore_wait(barrier, len(peers))


def gather_kernel(
    group, cycle, qd_ref, stats_ref, kv_ref, run_ref, qd_out, stats_out, kv_out, run_out,
    own_sem, kv_send, kv_recv, qd_send, qd_recv, st_send, st_recv, run_send, run_recv,
    ring_send, ring_recv, core_send, core_recv,
):
    digits = digits_of(cycle)
    head, ctx = lax.axis_index("head"), lax.axis_index("ctx")
    place = split_index(ctx, digits)
    half = group // 2
    each = qd_ref.shape[0] // group
    core = lax.rem(head, 2)
    sibling = head + 1 - 2 * core
    ahead = [lax.rem(head + k, group) for k in range(group)]
    behind = [lax.rem(head + group - k, group) for k in range(group)]
    ctx_ahead = [lax.rem(ctx + k, cycle) for k in range(cycle)]
    ctx_behind = [lax.rem(ctx + cycle - k, cycle) for k in range(cycle)]
    greet([(h, ctx) for h in ahead[1:]] + [(head, c) for c in ctx_ahead[1:]])

    def remote(src, dst, send, recv, to):
        return pltpu.make_async_remote_copy(
            src_ref=src, dst_ref=dst, send_sem=send, recv_sem=recv, device_id=to, device_id_type=MESH
        )

    started = []

    def start(copy):
        copy.start()
        started.append(copy)

    for k in range(1, group):
        start(remote(kv_ref, kv_out.at[ctx * group + head], kv_send.at[k], kv_recv.at[k], (ahead[k], ctx)))
    for k in range(1, cycle):
        start(remote(run_ref, run_out.at[ctx], run_send.at[k], run_recv.at[k], (head, ctx_ahead[k])))
    for k in range(1, group):
        rows = pl.ds(ahead[k] * each, each)
        start(remote(stats_ref.at[rows], stats_out.at[head], st_send.at[k], st_recv.at[k], (ahead[k], ctx)))
        start(remote(qd_ref.at[rows], qd_out.at[:, head], qd_send.at[k], qd_recv.at[k], (ahead[k], ctx)))
    mine = pl.ds(head * each, each)
    local_copies = [
        pltpu.make_async_copy(kv_ref, kv_out.at[ctx * group + head], own_sem.at[0]),
        pltpu.make_async_copy(run_ref, run_out.at[ctx], own_sem.at[1]),
        pltpu.make_async_copy(stats_ref.at[mine], stats_out.at[head], own_sem.at[2]),
        pltpu.make_async_copy(qd_ref.at[mine], qd_out.at[:, head], own_sem.at[3]),
    ]
    for copy in local_copies:
        copy.start()

    local_copies[0].wait()
    for k in range(1, group):
        remote(
            kv_ref, kv_out.at[ctx * group + behind[k]], kv_send.at[k], kv_recv.at[k], (behind[k], ctx)
        ).wait_recv()

    def region(label, owner):
        at = [lax.rem(p + n - o, n) for p, n, o in zip(place, digits, label)]
        return kv_out.at[pl.ds(join_index(at, digits) * group + owner * half, half)]

    def forward(label, level):
        block = region(label, core)
        for axis in range(level, len(digits)):
            for k in range(1, digits[axis]):
                to = list(place)
                to[axis] = lax.rem(place[axis] + k, digits[axis])
                farther = list(label)
                farther[axis] = k
                slot = join_index(farther, digits)
                start(
                    remote(
                        block, block, ring_send.at[slot], ring_recv.at[slot], (head, join_index(to, digits))
                    )
                )
        return block

    none = [0] * len(digits)
    forward(none, 0)
    labels = []
    held = [none]
    for axis in range(len(digits)):
        fresh = []
        for label in held:
            for k in range(1, digits[axis]):
                farther = list(label)
                farther[axis] = k
                fresh.append((farther, axis))
        labels += fresh
        held = held + [label for label, _ in fresh]
    for label, axis in labels:
        slot = join_index(label, digits)
        block = region(label, core)
        remote(block, block, ring_send.at[slot], ring_recv.at[slot], (head, ctx)).wait_recv()
        forward(label, axis + 1)
        start(remote(block, block, core_send.at[slot], core_recv.at[slot], (sibling, ctx)))
    for label, axis in labels:
        slot = join_index(label, digits)
        block = region(label, 1 - core)
        remote(block, block, core_send.at[slot], core_recv.at[slot], (sibling, ctx)).wait_recv()

    for k in range(1, cycle):
        remote(
            run_ref, run_out.at[ctx_behind[k]], run_send.at[k], run_recv.at[k], (head, ctx_behind[k])
        ).wait_recv()
    for k in range(1, group):
        to = (behind[k], ctx)
        remote(
            stats_ref.at[mine], stats_out.at[behind[k]], st_send.at[k], st_recv.at[k], to
        ).wait_recv()
        remote(
            qd_ref.at[mine], qd_out.at[:, behind[k]], qd_send.at[k], qd_recv.at[k], to
        ).wait_recv()
    for copy in local_copies[1:]:
        copy.wait()
    for copy in started:
        copy.wait_send()


def gather(group, cycle, qd, stats, kv, run):
    rows, wide = kv.shape
    each = qd.shape[0] // group
    whole = pl.BlockSpec(memory_space=pltpu.VMEM)
    dma = pltpu.SemaphoreType.DMA
    return pl.pallas_call(
        functools.partial(gather_kernel, group, cycle),
        out_shape=(
            jax.ShapeDtypeStruct((each, group, rows, wide), qd.dtype),
            jax.ShapeDtypeStruct((group, each) + stats.shape[1:], stats.dtype),
            jax.ShapeDtypeStruct((cycle * group, rows, wide), kv.dtype),
            jax.ShapeDtypeStruct((cycle,) + run.shape, run.dtype),
        ),
        in_specs=[whole] * 4,
        out_specs=(whole,) * 4,
        scratch_shapes=[dma((4,))]
        + [dma((group,))] * 6
        + [dma((cycle,))] * 6,
        compiler_params=pltpu.CompilerParams(
            collective_id=0, has_side_effects=True, vmem_limit_bytes=40 * 1024 * 1024
        ),
    )(qd, stats, kv, run)


def reduce_kernel(
    group, cycle, dq_ref, dkv_ref, dq_out, dk_out, dv_out,
    core_out, core_in, ring_out, ring_in, last, share,
    own_sem, dq_send, dq_recv, core_send, core_recv, ring_send, ring_recv, end_send, end_recv,
):
    digits = digits_of(cycle)
    levels = len(digits)
    head, ctx = lax.axis_index("head"), lax.axis_index("ctx")
    place = split_index(ctx, digits)
    half = group // 2
    each = dq_ref.shape[0]
    width = dk_out.shape[1]
    core, chip = lax.rem(head, 2), lax.div(head, 2)
    sibling = head + 1 - 2 * core
    ahead = [lax.rem(head + k, group) for k in range(group)]
    behind = [lax.rem(head + group - k, group) for k in range(group)]

    def moved(axis, k):
        to = list(place)
        to[axis] = lax.rem(place[axis] + k, digits[axis])
        return join_index(to, digits)

    greet(
        [(h, ctx) for h in ahead[1:]]
        + [(head, moved(axis, k)) for axis in range(levels) for k in range(1, digits[axis])]
    )

    def remote(src, dst, send, recv, to):
        return pltpu.make_async_remote_copy(
            src_ref=src, dst_ref=dst, send_sem=send, recv_sem=recv, device_id=to, device_id_type=MESH
        )

    started = []

    def start(copy):
        copy.start()
        started.append(copy)

    labels = [[]]
    for size in digits:
        labels = [label + [k] for label in labels for k in range(size)]
    slot_of = lambda label: join_index(label, digits)

    def level_of(label):
        moving = [axis for axis in range(levels) if label[axis]]
        return moving[-1] if moving else -1

    labels.sort(key=lambda label: -level_of(label))

    def terms(label, owner):
        at = [lax.rem(p + o, n) for p, n, o in zip(place, digits, label)]
        return dkv_ref[pl.ds(join_index(at, digits) * group + owner * half, half)]

    for label in labels:
        slot = slot_of(label)
        core_out[slot] = terms(label, 1 - core).astype(jnp.bfloat16)
        start(
            remote(
                core_out.at[slot], core_in.at[slot], core_send.at[slot], core_recv.at[slot], (sibling, ctx)
            )
        )
    for k in range(1, group):
        start(
            remote(
                dq_ref.at[:, ahead[k]],
                dq_out.at[pl.ds(head * each, each)],
                dq_send.at[k],
                dq_recv.at[k],
                (ahead[k], ctx),
            )
        )
    own = pltpu.make_async_copy(dq_ref.at[:, head], dq_out.at[pl.ds(head * each, each)], own_sem.at[0])
    own.start()

    for label in labels:
        slot = slot_of(label)
        remote(
            core_out.at[slot], core_in.at[slot], core_send.at[slot], core_recv.at[slot], (sibling, ctx)
        ).wait_recv()
        total = terms(label, core) + core_in[slot].astype(jnp.float32)
        level = level_of(label)
        for axis in range(levels - 1, level, -1):
            for k in range(1, digits[axis]):
                came = list(label)
                came[axis] = k
                at = slot_of(came)
                remote(
                    ring_out.at[at], ring_in.at[at], ring_send.at[at], ring_recv.at[at], (head, ctx)
                ).wait_recv()
                total = total + ring_in[at].astype(jnp.float32)
        if level >= 0:
            ring_out[slot] = total.astype(jnp.bfloat16)
            to = (head, moved(level, label[level]))
            start(remote(ring_out.at[slot], ring_in.at[slot], ring_send.at[slot], ring_recv.at[slot], to))
        else:
            share[...] = total

    for j in range(half):
        owner = core * half + j

        @pl.when(owner != head)
        def _():
            remote(
                share.at[j], last.at[chip], end_send.at[j], end_recv.at[chip], (owner, ctx)
            ).start()

        @pl.when(owner == head)
        def _():
            last[chip] = share[j]

    my_half = lax.div(head, half)
    for i in range(half):
        source = i * 2 + my_half

        @pl.when(source != head)
        def _():
            remote(
                share.at[0], last.at[i], end_send.at[0], end_recv.at[i], (source, ctx)
            ).wait_recv()

    total = last[0]
    for i in range(1, half):
        total = total + last[i]
    dk_out[...] = total[:, :width].astype(dk_out.dtype)
    dv_out[...] = total[:, width:].astype(dv_out.dtype)

    for k in range(1, group):
        remote(
            dq_ref.at[:, head],
            dq_out.at[pl.ds(behind[k] * each, each)],
            dq_send.at[k],
            dq_recv.at[k],
            (behind[k], ctx),
        ).wait_recv()
    own.wait()
    for copy in started:
        copy.wait_send()
    for j in range(half):
        owner = core * half + j

        @pl.when(owner != head)
        def _():
            remote(
                share.at[j], last.at[chip], end_send.at[j], end_recv.at[chip], (owner, ctx)
            ).wait_send()


def reduce_scatter(group, cycle, dq, dkv):
    each, _, rows, width = dq.shape
    wide = dkv.shape[2]
    half = group // 2
    whole = pl.BlockSpec(memory_space=pltpu.VMEM)
    dma = pltpu.SemaphoreType.DMA
    low = pltpu.VMEM((cycle, half, rows, wide), jnp.bfloat16)
    return pl.pallas_call(
        functools.partial(reduce_kernel, group, cycle),
        out_shape=(
            jax.ShapeDtypeStruct((each * group, rows, width), jnp.bfloat16),
            jax.ShapeDtypeStruct((rows, width), jnp.bfloat16),
            jax.ShapeDtypeStruct((rows, width), jnp.bfloat16),
        ),
        in_specs=[whole] * 2,
        out_specs=(whole,) * 3,
        scratch_shapes=[
            low,
            low,
            low,
            low,
            pltpu.VMEM((half, rows, wide), jnp.float32),
            pltpu.VMEM((half, rows, wide), jnp.float32),
            dma((1,)),
            dma((group,)),
            dma((group,)),
            dma((cycle,)),
            dma((cycle,)),
            dma((cycle,)),
            dma((cycle,)),
            dma((half,)),
            dma((half,)),
        ],
        compiler_params=pltpu.CompilerParams(
            collective_id=1, has_side_effects=True, vmem_limit_bytes=56 * 1024 * 1024
        ),
    )(dq, dkv)


def local(queries, key_rows, value_rows, attn_output, grad_output, logsumexp, positions):
    cycle = lax.axis_size("ctx")
    group = lax.axis_size("head")
    width = queries.shape[2]
    part = positions.shape[0]
    rows = part * group
    run = rows // 2
    heads = queries.shape[0] // group
    row_delta = jnp.sum(grad_output.astype(jnp.float32) * attn_output.astype(jnp.float32), axis=2)
    kv = jnp.concatenate([key_rows, value_rows], axis=1)
    qd = jnp.concatenate([queries, grad_output], axis=2)
    stats = jnp.stack([logsumexp, row_delta], axis=1)
    place = positions[0] // run
    low_run = jnp.where(lax.axis_index("head") < group // 2, place, 2 * cycle - 1 - place)
    qd, stats, kv, runs = gather(group, cycle, qd, stats, kv, jnp.full((8, 128), low_run, jnp.int32))
    stats = stats.reshape(2, group // 2, heads, 2, part).transpose(3, 0, 2, 1, 4)
    stats = stats.reshape(2, 2, 1, heads * run)
    mine = lax.axis_index("ctx").reshape(1)
    dq, dkv = tiles(
        cycle,
        runs[:, 0, 0],
        mine,
        qd.reshape(heads, rows, 2 * width),
        stats[0],
        stats[1],
        kv.reshape(cycle * rows, 2 * width),
    )
    return reduce_scatter(
        group,
        cycle,
        dq.reshape(heads, group, part, width),
        dkv.reshape(cycle * group, part, 2 * width),
    )


def solution(mesh):
    return jax.shard_map(
        local,
        mesh=mesh,
        in_specs=(
            P(None, ("ctx", "head"), None),
            P(("ctx", "head"), None),
            P(("ctx", "head"), None),
            P(None, ("ctx", "head"), None),
            P(None, ("ctx", "head"), None),
            P(None, ("ctx", "head")),
            P(("ctx", "head")),
        ),
        out_specs=(
            P(None, ("ctx", "head"), None),
            P(("ctx", "head"), None),
            P(("ctx", "head"), None),
        ),
        check_vma=False,
    )
```

```python
import functools
import math

import jax
import jax.numpy as jnp
from jax import lax
from jax.experimental import pallas as pl
from jax.experimental.pallas import tpu as pltpu
from jax.sharding import PartitionSpec as P


def contract(a, b, axes):
    return lax.dot_general(a, b, (axes, ((), ())), preferred_element_type=jnp.float32)


MESH = pl.DeviceIdType.MESH


def digits_of(cycle):
    return {8: (4, 2), 32: (4, 4, 2)}.get(cycle, (cycle,))


def split_index(index, digits):
    parts = []
    for size in reversed(digits):
        parts.append(lax.rem(index, size))
        index = lax.div(index, size)
    return parts[::-1]


def join_index(parts, digits):
    index = 0
    for part, size in zip(parts, digits):
        index = index * size + part
    return index


def greet(peers):
    barrier = pltpu.get_barrier_semaphore()
    for head, ctx in peers:
        pl.semaphore_signal(barrier, inc=1, device_id=(head, ctx), device_id_type=MESH)
    pl.semaphore_wait(barrier, len(peers))


def gather_kernel(
    group, cycle, qd_ref, stats_ref, kv_ref, run_ref, qd_out, stats_out, kv_out, run_out,
    own_sem, kv_send, kv_recv, qd_send, qd_recv, st_send, st_recv, run_send, run_recv,
    ring_send, ring_recv, core_send, core_recv,
):
    digits = digits_of(cycle)
    head, ctx = lax.axis_index("head"), lax.axis_index("ctx")
    place = split_index(ctx, digits)
    half = group // 2
    each = qd_ref.shape[0] // group
    core = lax.rem(head, 2)
    sibling = head + 1 - 2 * core
    ahead = [lax.rem(head + k, group) for k in range(group)]
    behind = [lax.rem(head + group - k, group) for k in range(group)]
    ctx_ahead = [lax.rem(ctx + k, cycle) for k in range(cycle)]
    ctx_behind = [lax.rem(ctx + cycle - k, cycle) for k in range(cycle)]
    greet([(h, ctx) for h in ahead[1:]] + [(head, c) for c in ctx_ahead[1:]])

    def remote(src, dst, send, recv, to):
        return pltpu.make_async_remote_copy(
            src_ref=src, dst_ref=dst, send_sem=send, recv_sem=recv, device_id=to, device_id_type=MESH
        )

    started = []

    def start(copy):
        copy.start()
        started.append(copy)

    for k in range(1, group):
        start(remote(kv_ref, kv_out.at[ctx * group + head], kv_send.at[k], kv_recv.at[k], (ahead[k], ctx)))
    for k in range(1, cycle):
        start(remote(run_ref, run_out.at[ctx], run_send.at[k], run_recv.at[k], (head, ctx_ahead[k])))
    for k in range(1, group):
        rows = pl.ds(ahead[k] * each, each)
        start(remote(stats_ref.at[rows], stats_out.at[head], st_send.at[k], st_recv.at[k], (ahead[k], ctx)))
        start(remote(qd_ref.at[rows], qd_out.at[:, head], qd_send.at[k], qd_recv.at[k], (ahead[k], ctx)))
    mine = pl.ds(head * each, each)
    local_copies = [
        pltpu.make_async_copy(kv_ref, kv_out.at[ctx * group + head], own_sem.at[0]),
        pltpu.make_async_copy(run_ref, run_out.at[ctx], own_sem.at[1]),
        pltpu.make_async_copy(stats_ref.at[mine], stats_out.at[head], own_sem.at[2]),
        pltpu.make_async_copy(qd_ref.at[mine], qd_out.at[:, head], own_sem.at[3]),
    ]
    for copy in local_copies:
        copy.start()

    local_copies[0].wait()
    for k in range(1, group):
        remote(
            kv_ref, kv_out.at[ctx * group + behind[k]], kv_send.at[k], kv_recv.at[k], (behind[k], ctx)
        ).wait_recv()

    def region(label, owner):
        at = [lax.rem(p + n - o, n) for p, n, o in zip(place, digits, label)]
        return kv_out.at[pl.ds(join_index(at, digits) * group + owner * half, half)]

    def forward(label, level):
        block = region(label, core)
        for axis in range(level, len(digits)):
            for k in range(1, digits[axis]):
                to = list(place)
                to[axis] = lax.rem(place[axis] + k, digits[axis])
                farther = list(label)
                farther[axis] = k
                slot = join_index(farther, digits)
                start(
                    remote(
                        block, block, ring_send.at[slot], ring_recv.at[slot], (head, join_index(to, digits))
                    )
                )
        return block

    none = [0] * len(digits)
    forward(none, 0)
    labels = []
    held = [none]
    for axis in range(len(digits)):
        fresh = []
        for label in held:
            for k in range(1, digits[axis]):
                farther = list(label)
                farther[axis] = k
                fresh.append((farther, axis))
        labels += fresh
        held = held + [label for label, _ in fresh]
    for label, axis in labels:
        slot = join_index(label, digits)
        block = region(label, core)
        remote(block, block, ring_send.at[slot], ring_recv.at[slot], (head, ctx)).wait_recv()
        forward(label, axis + 1)
        start(remote(block, block, core_send.at[slot], core_recv.at[slot], (sibling, ctx)))
    for label, axis in labels:
        slot = join_index(label, digits)
        block = region(label, 1 - core)
        remote(block, block, core_send.at[slot], core_recv.at[slot], (sibling, ctx)).wait_recv()

    for k in range(1, cycle):
        remote(
            run_ref, run_out.at[ctx_behind[k]], run_send.at[k], run_recv.at[k], (head, ctx_behind[k])
        ).wait_recv()
    for k in range(1, group):
        to = (behind[k], ctx)
        remote(
            stats_ref.at[mine], stats_out.at[behind[k]], st_send.at[k], st_recv.at[k], to
        ).wait_recv()
        remote(
            qd_ref.at[mine], qd_out.at[:, behind[k]], qd_send.at[k], qd_recv.at[k], to
        ).wait_recv()
    for copy in local_copies[1:]:
        copy.wait()
    for copy in started:
        copy.wait_send()


def gather(group, cycle, qd, stats, kv, run):
    rows, wide = kv.shape
    each = qd.shape[0] // group
    whole = pl.BlockSpec(memory_space=pltpu.VMEM)
    dma = pltpu.SemaphoreType.DMA
    return pl.pallas_call(
        functools.partial(gather_kernel, group, cycle),
        out_shape=(
            jax.ShapeDtypeStruct((each, group, rows, wide), qd.dtype),
            jax.ShapeDtypeStruct((group, each) + stats.shape[1:], stats.dtype),
            jax.ShapeDtypeStruct((cycle * group, rows, wide), kv.dtype),
            jax.ShapeDtypeStruct((cycle,) + run.shape, run.dtype),
        ),
        in_specs=[whole] * 4,
        out_specs=(whole,) * 4,
        scratch_shapes=[dma((4,))]
        + [dma((group,))] * 6
        + [dma((cycle,))] * 6,
        compiler_params=pltpu.CompilerParams(
            collective_id=0, has_side_effects=True, vmem_limit_bytes=40 * 1024 * 1024
        ),
    )(qd, stats, kv, run)


def backward_kernel(
    group, cycle, late_ref, qd_ref, lse_ref, delta_ref, kv_ref, dq_out, sums_out,
    acc, pair, dq, own, core_out, core_in, ring_out, ring_in, last, share,
    own_sem, dq_send, dq_recv, core_send, core_recv, ring_send, ring_recv, end_send, end_recv,
):
    digits = digits_of(cycle)
    levels = len(digits)
    head, ctx = lax.axis_index("head"), lax.axis_index("ctx")
    place = split_index(ctx, digits)
    half = group // 2
    heads, rows, wide = qd_ref.shape
    width = wide // 2
    run = rows // 2
    part = rows // group
    scaling = width ** (-0.5)
    log2e = 1.0 / math.log(2.0)
    core, chip = lax.rem(head, 2), lax.div(head, 2)
    sibling = head + 1 - 2 * core
    ahead = [lax.rem(head + k, group) for k in range(group)]
    behind = [lax.rem(head + group - k, group) for k in range(group)]

    def moved(axis, k):
        to = list(place)
        to[axis] = lax.rem(place[axis] + k, digits[axis])
        return join_index(to, digits)

    greet(
        [(h, ctx) for h in ahead[1:]]
        + [(head, moved(axis, k)) for axis in range(levels) for k in range(1, digits[axis])]
    )

    def remote(src, dst, send, recv, to):
        return pltpu.make_async_remote_copy(
            src_ref=src, dst_ref=dst, send_sem=send, recv_sem=recv, device_id=to, device_id_type=MESH
        )

    acc[...] = jnp.zeros_like(acc)

    def stats_of(ref, query_half, goes):
        if query_half is not None:
            return ref[query_half]
        return jnp.where(goes, ref[1], ref[0])

    def unit(query_half, first, key_half, diagonal, late=None):
        def rows_of(at):
            return slice(at * run, (at + 1) * run)

        def keys_of(at):
            return pl.ds(pl.multiple_of(first + at * run, run), run)

        if late is None:
            goes = None
            query = qd_ref[:, rows_of(query_half), :width].reshape(heads * run, width)
            grad = qd_ref[:, rows_of(query_half), width:].reshape(heads * run, width)
            key = kv_ref[keys_of(key_half), :width]
            value = kv_ref[keys_of(key_half), width:]
        else:
            goes = late > 0.5

            def chosen(early_value, late_value):
                flag = jnp.broadcast_to(late[:, :width], early_value.shape).astype(jnp.bfloat16)
                return late_value * flag + early_value * (1 - flag)

            query, grad = (
                chosen(
                    qd_ref[:, rows_of(0), columns].reshape(heads * run, width),
                    qd_ref[:, rows_of(1), columns].reshape(heads * run, width),
                )
                for columns in (slice(0, width), slice(width, wide))
            )
            key, value = (
                chosen(kv_ref[keys_of(0), columns], kv_ref[keys_of(1), columns])
                for columns in (slice(0, width), slice(width, wide))
            )
        scores = contract(key, query, ((1,), (1,)))
        prob = jnp.exp2(scores * (scaling * log2e) - stats_of(lse_ref, query_half, goes) * log2e)
        if diagonal:
            key_at = lax.broadcasted_iota(jnp.int32, scores.shape, 0)
            query_at = lax.broadcasted_iota(jnp.int32, scores.shape, 1) % run
            prob = jnp.where(key_at <= query_at, prob, 0.0)
        grad_prob = contract(value, grad, ((1,), (1,)))
        grad_score = (prob * (grad_prob - stats_of(delta_ref, query_half, goes))).astype(jnp.bfloat16)
        value_grad = contract(prob.astype(jnp.bfloat16), grad, ((1,), (0,)))
        key_grad = contract(grad_score, query, ((1,), (0,)))
        query_grad = contract(key.T, grad_score, ((1,), (0,)))
        return query_grad, key_grad * scaling, value_grad

    def by_owner(terms):
        return terms.reshape(half, part, width)

    def label_of(level, number):
        label = [0] * levels
        label[level] = lax.rem(number, digits[level] - 1) + 1
        number = lax.div(number, digits[level] - 1)
        for axis in range(level - 1, -1, -1):
            label[axis] = lax.rem(number, digits[axis])
            number = lax.div(number, digits[axis])
        return label

    def to_sibling(slot):
        return remote(
            core_out.at[slot], core_in.at[slot], core_send.at[slot], core_recv.at[slot], (sibling, ctx)
        )

    def hand_over(slot):
        core_out[slot] = pair[1 - core].astype(jnp.bfloat16)
        own[slot] = pair[core]
        to_sibling(slot).start()

    def along(slot, to):
        return remote(ring_out.at[slot], ring_in.at[slot], ring_send.at[slot], ring_recv.at[slot], to)

    def combined(label, level):
        slot = join_index(label, digits)
        to_sibling(slot).wait_recv()
        total = own[slot] + core_in[slot].astype(jnp.float32)
        for axis in range(levels - 1, level, -1):
            for k in range(1, digits[axis]):
                came = list(label)
                came[axis] = k
                at = join_index(came, digits)
                along(at, (head, ctx)).wait_recv()
                total = total + ring_in[at].astype(jnp.float32)
        return slot, total

    def pass_on(label, level):
        slot, total = combined(label, level)
        ring_out[slot] = total.astype(jnp.bfloat16)
        to = list(place)
        to[level] = lax.rem(place[level] + label[level], digits[level])
        along(slot, (head, join_index(to, digits))).start()

    def count_of(level):
        return math.prod(digits[:level]) * (digits[level] - 1)

    for level in range(levels - 1, -1, -1):

        @pl.loop(0, count_of(level))
        def _(number):
            label = label_of(level, number)
            at = [lax.rem(p + o, n) for p, n, o in zip(place, digits, label)]
            other = join_index(at, digits)
            first = other * rows
            late = late_ref[other]
            query_grad, key_grad, value_grad = unit(1, first, 0, False)
            acc[1] += query_grad
            pair[0, :, :, :width] = by_owner(key_grad)
            pair[0, :, :, width:] = by_owner(value_grad)
            query_grad, key_grad, value_grad = unit(None, first, None, False, late)
            goes = jnp.broadcast_to(late, query_grad.shape) > 0.5
            acc[0] += jnp.where(goes, 0.0, query_grad)
            acc[1] += jnp.where(goes, query_grad, 0.0)
            goes = jnp.broadcast_to(late[:, :width], key_grad.shape) > 0.5
            pair[0, :, :, :width] += by_owner(jnp.where(goes, 0.0, key_grad))
            pair[0, :, :, width:] += by_owner(jnp.where(goes, 0.0, value_grad))
            pair[1, :, :, :width] = by_owner(jnp.where(goes, key_grad, 0.0))
            pair[1, :, :, width:] = by_owner(jnp.where(goes, value_grad, 0.0))
            hand_over(join_index(label, digits))

            @pl.when(number > 0)
            def _():
                pass_on(label_of(level, number - 1), level)

            if level < levels - 1:

                @pl.when(number == 0)
                def _():
                    pass_on(label_of(level + 1, count_of(level + 1) - 1), level + 1)

    first = ctx * rows
    query_grad, key_grad, value_grad = unit(1, first, 0, False)
    acc[1] += query_grad
    pair[0, :, :, :width] = by_owner(key_grad)
    pair[0, :, :, width:] = by_owner(value_grad)
    pass_on(label_of(0, count_of(0) - 1), 0)
    query_grad, key_grad, value_grad = unit(0, first, 0, True)
    acc[0] += query_grad
    pair[0, :, :, :width] += by_owner(key_grad)
    pair[0, :, :, width:] += by_owner(value_grad)
    query_grad, key_grad, value_grad = unit(1, first, 1, True)
    acc[1] += query_grad
    pair[1, :, :, :width] = by_owner(key_grad)
    pair[1, :, :, width:] = by_owner(value_grad)
    hand_over(0)

    for at in range(2):
        for h in range(heads):
            turned = (acc[at, :, h * run : (h + 1) * run] * scaling).T.astype(jnp.bfloat16)
            dq[h, at * half : (at + 1) * half] = turned.reshape(half, part, width)

    def query_copy(k, block, to):
        return remote(
            dq.at[:, block], dq_out.at[pl.ds(to[1] * heads, heads)], dq_send.at[k], dq_recv.at[k], (to[0], ctx)
        )

    for k in range(1, group):
        query_copy(k, ahead[k], (ahead[k], head)).start()
    stay = pltpu.make_async_copy(dq.at[:, head], dq_out.at[pl.ds(head * heads, heads)], own_sem.at[0])
    stay.start()

    share[...] = combined([0] * levels, -1)[1]
    for j in range(half):
        owner = core * half + j

        @pl.when(owner != head)
        def _():
            remote(
                share.at[j], last.at[chip], end_send.at[j], end_recv.at[chip], (owner, ctx)
            ).start()

        @pl.when(owner == head)
        def _():
            last[chip] = share[j]

    my_half = lax.div(head, half)
    for i in range(half):
        source = i * 2 + my_half

        @pl.when(source != head)
        def _():
            remote(
                share.at[0], last.at[i], end_send.at[0], end_recv.at[i], (source, ctx)
            ).wait_recv()

    total = last[0]
    for i in range(1, half):
        total = total + last[i]
    sums_out[...] = total

    for k in range(1, group):
        query_copy(k, head, (behind[k], behind[k])).wait_recv()
    stay.wait()
    for k in range(1, group):
        query_copy(k, ahead[k], (ahead[k], head)).wait_send()
    for slot in range(cycle):
        to_sibling(slot).wait_send()
        if slot:
            along(slot, (head, ctx)).wait_send()
    for j in range(half):
        owner = core * half + j

        @pl.when(owner != head)
        def _():
            remote(
                share.at[j], last.at[chip], end_send.at[j], end_recv.at[chip], (owner, ctx)
            ).wait_send()


def backward(group, cycle, late, qd, lse, delta, kv):
    heads, rows, wide = qd.shape
    width = wide // 2
    part = rows // group
    half = group // 2
    whole = pl.BlockSpec(memory_space=pltpu.VMEM)
    dma = pltpu.SemaphoreType.DMA
    low = pltpu.VMEM((cycle, half, part, wide), jnp.bfloat16)
    ends = pltpu.VMEM((half, part, wide), jnp.float32)
    return pl.pallas_call(
        functools.partial(backward_kernel, group, cycle),
        out_shape=(
            jax.ShapeDtypeStruct((heads * group, part, width), jnp.bfloat16),
            jax.ShapeDtypeStruct((part, wide), jnp.float32),
        ),
        in_specs=[whole] * 5,
        out_specs=(whole,) * 2,
        scratch_shapes=[
            pltpu.VMEM((2, width, heads * rows // 2), jnp.float32),
            pltpu.VMEM((2, half, part, wide), jnp.float32),
            pltpu.VMEM((heads, group, part, width), jnp.bfloat16),
            pltpu.VMEM((cycle, half, part, wide), jnp.float32),
            low,
            low,
            low,
            low,
            ends,
            ends,
            dma((1,)),
            dma((group,)),
            dma((group,)),
            dma((cycle,)),
            dma((cycle,)),
            dma((cycle,)),
            dma((cycle,)),
            dma((half,)),
            dma((half,)),
        ],
        compiler_params=pltpu.CompilerParams(
            collective_id=1, has_side_effects=True, vmem_limit_bytes=58 * 1024 * 1024
        ),
    )(late, qd, lse, delta, kv)


def local(queries, key_rows, value_rows, attn_output, grad_output, logsumexp, positions):
    cycle = lax.axis_size("ctx")
    group = lax.axis_size("head")
    width = queries.shape[2]
    part = positions.shape[0]
    rows = part * group
    run = rows // 2
    heads = queries.shape[0] // group
    row_delta = jnp.sum(grad_output.astype(jnp.float32) * attn_output.astype(jnp.float32), axis=2)
    kv = jnp.concatenate([key_rows, value_rows], axis=1)
    qd = jnp.concatenate([queries, grad_output], axis=2)
    stats = jnp.stack([logsumexp, row_delta], axis=1)
    place = positions[0] // run
    low_run = jnp.where(lax.axis_index("head") < group // 2, place, 2 * cycle - 1 - place)
    qd, stats, kv, runs = gather(group, cycle, qd, stats, kv, jnp.full((8, 128), low_run, jnp.int32))
    stats = stats.reshape(2, group // 2, heads, 2, part).transpose(3, 0, 2, 1, 4)
    stats = stats.reshape(2, 2, 1, heads * run)
    runs = runs[:, 0, 0]
    late = (runs > low_run).astype(jnp.float32)
    late = jnp.broadcast_to(late[:, None, None], (cycle, 1, heads * run))
    grad_queries, sums = backward(
        group,
        cycle,
        late,
        qd.reshape(heads, rows, 2 * width),
        stats[0],
        stats[1],
        kv.reshape(cycle * rows, 2 * width),
    )
    return grad_queries, sums[:, :width].astype(jnp.bfloat16), sums[:, width:].astype(jnp.bfloat16)


def solution(mesh):
    return jax.shard_map(
        local,
        mesh=mesh,
        in_specs=(
            P(None, ("ctx", "head"), None),
            P(("ctx", "head"), None),
            P(("ctx", "head"), None),
            P(None, ("ctx", "head"), None),
            P(None, ("ctx", "head"), None),
            P(None, ("ctx", "head")),
            P(("ctx", "head")),
        ),
        out_specs=(
            P(None, ("ctx", "head"), None),
            P(("ctx", "head"), None),
            P(("ctx", "head"), None),
        ),
        check_vma=False,
    )
```

```python
import functools
import math

import jax
import jax.numpy as jnp
from jax import lax
from jax.experimental import pallas as pl
from jax.experimental.pallas import tpu as pltpu
from jax.sharding import PartitionSpec as P


def contract(a, b, axes):
    return lax.dot_general(a, b, (axes, ((), ())), preferred_element_type=jnp.float32)


MESH = pl.DeviceIdType.MESH


def digits_of(cycle):
    return {8: (4, 2), 32: (4, 4, 2)}.get(cycle, (cycle,))


def split_index(index, digits):
    parts = []
    for size in reversed(digits):
        parts.append(lax.rem(index, size))
        index = lax.div(index, size)
    return parts[::-1]


def join_index(parts, digits):
    index = 0
    for part, size in zip(parts, digits):
        index = index * size + part
    return index


def greet(peers):
    barrier = pltpu.get_barrier_semaphore()
    for head, ctx in peers:
        pl.semaphore_signal(barrier, inc=1, device_id=(head, ctx), device_id_type=MESH)
    pl.semaphore_wait(barrier, len(peers))


def gather_kernel(
    group, cycle, query_ref, grad_ref, output_ref, lse_ref, key_ref, value_ref, run_ref,
    qd_out, stats_out, kv_out, run_out, stats_ref,
    own_sem, kv_send, kv_recv, qd_send, qd_recv, st_send, st_recv, run_send, run_recv,
    ring_send, ring_recv, core_send, core_recv,
):
    digits = digits_of(cycle)
    head, ctx = lax.axis_index("head"), lax.axis_index("ctx")
    place = split_index(ctx, digits)
    half = group // 2
    each = query_ref.shape[0] // group
    width = query_ref.shape[2]
    columns = (slice(0, width), slice(width, 2 * width))
    core = lax.rem(head, 2)
    sibling = head + 1 - 2 * core
    ahead = [lax.rem(head + k, group) for k in range(group)]
    behind = [lax.rem(head + group - k, group) for k in range(group)]
    ctx_ahead = [lax.rem(ctx + k, cycle) for k in range(cycle)]
    ctx_behind = [lax.rem(ctx + cycle - k, cycle) for k in range(cycle)]
    greet([(h, ctx) for h in ahead[1:]] + [(head, c) for c in ctx_ahead[1:]])

    def remote(src, dst, send, recv, to):
        return pltpu.make_async_remote_copy(
            src_ref=src, dst_ref=dst, send_sem=send, recv_sem=recv, device_id=to, device_id_type=MESH
        )

    started = []

    def start(copy):
        copy.start()
        started.append(copy)

    for k in range(1, group):
        for n, ref in enumerate((key_ref, value_ref)):
            to = kv_out.at[ctx * group + head, :, columns[n]]
            start(remote(ref, to, kv_send.at[n, k], kv_recv.at[n, k], (ahead[k], ctx)))
    for k in range(1, cycle):
        start(remote(run_ref, run_out.at[ctx], run_send.at[k], run_recv.at[k], (head, ctx_ahead[k])))
    for k in range(1, group):
        rows = pl.ds(ahead[k] * each, each)
        for n, ref in enumerate((query_ref, grad_ref)):
            to = qd_out.at[:, head, :, columns[n]]
            start(remote(ref.at[rows], to, qd_send.at[n, k], qd_recv.at[n, k], (ahead[k], ctx)))
    mine = pl.ds(head * each, each)
    here = kv_out.at[ctx * group + head]
    local_copies = [
        pltpu.make_async_copy(key_ref, here.at[:, columns[0]], own_sem.at[0]),
        pltpu.make_async_copy(value_ref, here.at[:, columns[1]], own_sem.at[1]),
        pltpu.make_async_copy(run_ref, run_out.at[ctx], own_sem.at[2]),
        pltpu.make_async_copy(query_ref.at[mine], qd_out.at[:, head, :, columns[0]], own_sem.at[3]),
        pltpu.make_async_copy(grad_ref.at[mine], qd_out.at[:, head, :, columns[1]], own_sem.at[4]),
    ]
    for copy in local_copies:
        copy.start()

    local_copies[0].wait()
    local_copies[1].wait()
    for k in range(1, group):
        for n, ref in enumerate((key_ref, value_ref)):
            to = kv_out.at[ctx * group + behind[k], :, columns[n]]
            remote(ref, to, kv_send.at[n, k], kv_recv.at[n, k], (behind[k], ctx)).wait_recv()

    def region(label, owner):
        at = [lax.rem(p + n - o, n) for p, n, o in zip(place, digits, label)]
        return kv_out.at[pl.ds(join_index(at, digits) * group + owner * half, half)]

    def forward(label, level):
        block = region(label, core)
        for axis in range(level, len(digits)):
            for k in range(1, digits[axis]):
                to = list(place)
                to[axis] = lax.rem(place[axis] + k, digits[axis])
                farther = list(label)
                farther[axis] = k
                slot = join_index(farther, digits)
                start(
                    remote(
                        block, block, ring_send.at[slot], ring_recv.at[slot], (head, join_index(to, digits))
                    )
                )
        return block

    none = [0] * len(digits)
    forward(none, 0)
    for h in range(query_ref.shape[0]):
        product = grad_ref[h].astype(jnp.float32) * output_ref[h].astype(jnp.float32)
        stats_ref[h, 0:1, :] = lse_ref[h : h + 1, :]
        stats_ref[h, 1:2, :] = jnp.sum(product.T, axis=0, keepdims=True)
    for k in range(1, group):
        rows = pl.ds(ahead[k] * each, each)
        start(remote(stats_ref.at[rows], stats_out.at[head], st_send.at[k], st_recv.at[k], (ahead[k], ctx)))
    stay = pltpu.make_async_copy(stats_ref.at[mine], stats_out.at[head], own_sem.at[5])
    stay.start()
    local_copies.append(stay)
    labels = []
    held = [none]
    for axis in range(len(digits)):
        fresh = []
        for label in held:
            for k in range(1, digits[axis]):
                farther = list(label)
                farther[axis] = k
                fresh.append((farther, axis))
        labels += fresh
        held = held + [label for label, _ in fresh]
    for label, axis in labels:
        slot = join_index(label, digits)
        block = region(label, core)
        remote(block, block, ring_send.at[slot], ring_recv.at[slot], (head, ctx)).wait_recv()
        forward(label, axis + 1)
        start(remote(block, block, core_send.at[slot], core_recv.at[slot], (sibling, ctx)))
    for label, axis in labels:
        slot = join_index(label, digits)
        block = region(label, 1 - core)
        remote(block, block, core_send.at[slot], core_recv.at[slot], (sibling, ctx)).wait_recv()

    for k in range(1, cycle):
        remote(
            run_ref, run_out.at[ctx_behind[k]], run_send.at[k], run_recv.at[k], (head, ctx_behind[k])
        ).wait_recv()
    for k in range(1, group):
        to = (behind[k], ctx)
        remote(
            stats_ref.at[mine], stats_out.at[behind[k]], st_send.at[k], st_recv.at[k], to
        ).wait_recv()
        for n, ref in enumerate((query_ref, grad_ref)):
            place_of = qd_out.at[:, behind[k], :, columns[n]]
            remote(ref.at[mine], place_of, qd_send.at[n, k], qd_recv.at[n, k], to).wait_recv()
    for copy in local_copies[2:]:
        copy.wait()
    for copy in started:
        copy.wait_send()


def gather(group, cycle, queries, grads, outputs, lse, keys, values, run):
    heads, rows, width = queries.shape
    each, wide = heads // group, 2 * width
    whole = pl.BlockSpec(memory_space=pltpu.VMEM)
    dma = pltpu.SemaphoreType.DMA
    return pl.pallas_call(
        functools.partial(gather_kernel, group, cycle),
        out_shape=(
            jax.ShapeDtypeStruct((each, group, rows, wide), queries.dtype),
            jax.ShapeDtypeStruct((group, each, 2, rows), jnp.float32),
            jax.ShapeDtypeStruct((cycle * group, rows, wide), keys.dtype),
            jax.ShapeDtypeStruct((cycle,) + run.shape, run.dtype),
        ),
        in_specs=[whole] * 7,
        out_specs=(whole,) * 4,
        scratch_shapes=[pltpu.VMEM((heads, 2, rows), jnp.float32), dma((6,))]
        + [dma((2, group))] * 4
        + [dma((group,))] * 2
        + [dma((cycle,))] * 6,
        compiler_params=pltpu.CompilerParams(
            collective_id=0, has_side_effects=True, vmem_limit_bytes=40 * 1024 * 1024
        ),
    )(queries, grads, outputs, lse, keys, values, run)


def backward_kernel(
    group, cycle, late_ref, qd_ref, lse_ref, delta_ref, kv_ref, dq_out, sums_out,
    acc, pair, dq, own, core_out, core_in, ring_out, ring_in, last, share,
    own_sem, dq_send, dq_recv, core_send, core_recv, ring_send, ring_recv, end_send, end_recv,
):
    digits = digits_of(cycle)
    levels = len(digits)
    head, ctx = lax.axis_index("head"), lax.axis_index("ctx")
    place = split_index(ctx, digits)
    half = group // 2
    heads, rows, wide = qd_ref.shape
    width = wide // 2
    run = rows // 2
    part = rows // group
    scaling = width ** (-0.5)
    log2e = 1.0 / math.log(2.0)
    core, chip = lax.rem(head, 2), lax.div(head, 2)
    sibling = head + 1 - 2 * core
    ahead = [lax.rem(head + k, group) for k in range(group)]
    behind = [lax.rem(head + group - k, group) for k in range(group)]

    def moved(axis, k):
        to = list(place)
        to[axis] = lax.rem(place[axis] + k, digits[axis])
        return join_index(to, digits)

    greet(
        [(h, ctx) for h in ahead[1:]]
        + [(head, moved(axis, k)) for axis in range(levels) for k in range(1, digits[axis])]
    )

    def remote(src, dst, send, recv, to):
        return pltpu.make_async_remote_copy(
            src_ref=src, dst_ref=dst, send_sem=send, recv_sem=recv, device_id=to, device_id_type=MESH
        )

    acc[...] = jnp.zeros_like(acc)

    def stats_of(ref, query_half, goes):
        if query_half is not None:
            return ref[query_half]
        return jnp.where(goes, ref[1], ref[0])

    def unit(query_half, first, key_half, diagonal, late=None):
        def rows_of(at):
            return slice(at * run, (at + 1) * run)

        def keys_of(at):
            return pl.ds(pl.multiple_of(first + at * run, run), run)

        if late is None:
            goes = None
            query = qd_ref[:, rows_of(query_half), :width].reshape(heads * run, width)
            grad = qd_ref[:, rows_of(query_half), width:].reshape(heads * run, width)
            key = kv_ref[keys_of(key_half), :width]
            value = kv_ref[keys_of(key_half), width:]
        else:
            goes = late > 0.5

            def chosen(early_value, late_value):
                flag = jnp.broadcast_to(late[:, :width], early_value.shape).astype(jnp.bfloat16)
                return late_value * flag + early_value * (1 - flag)

            query, grad = (
                chosen(
                    qd_ref[:, rows_of(0), columns].reshape(heads * run, width),
                    qd_ref[:, rows_of(1), columns].reshape(heads * run, width),
                )
                for columns in (slice(0, width), slice(width, wide))
            )
            key, value = (
                chosen(kv_ref[keys_of(0), columns], kv_ref[keys_of(1), columns])
                for columns in (slice(0, width), slice(width, wide))
            )
        scores = contract(key, query, ((1,), (1,)))
        prob = jnp.exp2(scores * (scaling * log2e) - stats_of(lse_ref, query_half, goes) * log2e)
        if diagonal:
            key_at = lax.broadcasted_iota(jnp.int32, scores.shape, 0)
            query_at = lax.broadcasted_iota(jnp.int32, scores.shape, 1) % run
            prob = jnp.where(key_at <= query_at, prob, 0.0)
        grad_prob = contract(value, grad, ((1,), (1,)))
        grad_score = (prob * (grad_prob - stats_of(delta_ref, query_half, goes))).astype(jnp.bfloat16)
        value_grad = contract(prob.astype(jnp.bfloat16), grad, ((1,), (0,)))
        key_grad = contract(grad_score, query, ((1,), (0,)))
        query_grad = contract(key.T, grad_score, ((1,), (0,)))
        return query_grad, key_grad * scaling, value_grad

    def by_owner(terms):
        return terms.reshape(half, part, width)

    def label_of(level, number):
        label = [0] * levels
        label[level] = lax.rem(number, digits[level] - 1) + 1
        number = lax.div(number, digits[level] - 1)
        for axis in range(level - 1, -1, -1):
            label[axis] = lax.rem(number, digits[axis])
            number = lax.div(number, digits[axis])
        return label

    def to_sibling(slot):
        return remote(
            core_out.at[slot], core_in.at[slot], core_send.at[slot], core_recv.at[slot], (sibling, ctx)
        )

    def hand_over(slot):
        core_out[slot] = pair[1 - core].astype(jnp.bfloat16)
        own[slot] = pair[core]
        to_sibling(slot).start()

    def along(slot, to):
        return remote(ring_out.at[slot], ring_in.at[slot], ring_send.at[slot], ring_recv.at[slot], to)

    def combined(label, level):
        slot = join_index(label, digits)
        to_sibling(slot).wait_recv()
        total = own[slot] + core_in[slot].astype(jnp.float32)
        for axis in range(levels - 1, level, -1):
            for k in range(1, digits[axis]):
                came = list(label)
                came[axis] = k
                at = join_index(came, digits)
                along(at, (head, ctx)).wait_recv()
                total = total + ring_in[at].astype(jnp.float32)
        return slot, total

    def pass_on(label, level):
        slot, total = combined(label, level)
        ring_out[slot] = total.astype(jnp.bfloat16)
        to = list(place)
        to[level] = lax.rem(place[level] + label[level], digits[level])
        along(slot, (head, join_index(to, digits))).start()

    def count_of(level):
        return math.prod(digits[:level]) * (digits[level] - 1)

    for level in range(levels - 1, -1, -1):

        @pl.loop(0, count_of(level))
        def _(number):
            label = label_of(level, number)
            at = [lax.rem(p + o, n) for p, n, o in zip(place, digits, label)]
            other = join_index(at, digits)
            first = other * rows
            late = late_ref[other]
            query_grad, key_grad, value_grad = unit(1, first, 0, False)
            acc[1] += query_grad
            pair[0, :, :, :width] = by_owner(key_grad)
            pair[0, :, :, width:] = by_owner(value_grad)
            query_grad, key_grad, value_grad = unit(None, first, None, False, late)
            goes = jnp.broadcast_to(late, query_grad.shape) > 0.5
            acc[0] += jnp.where(goes, 0.0, query_grad)
            acc[1] += jnp.where(goes, query_grad, 0.0)
            goes = jnp.broadcast_to(late[:, :width], key_grad.shape) > 0.5
            pair[0, :, :, :width] += by_owner(jnp.where(goes, 0.0, key_grad))
            pair[0, :, :, width:] += by_owner(jnp.where(goes, 0.0, value_grad))
            pair[1, :, :, :width] = by_owner(jnp.where(goes, key_grad, 0.0))
            pair[1, :, :, width:] = by_owner(jnp.where(goes, value_grad, 0.0))
            hand_over(join_index(label, digits))

            @pl.when(number > 0)
            def _():
                pass_on(label_of(level, number - 1), level)

            if level < levels - 1:

                @pl.when(number == 0)
                def _():
                    pass_on(label_of(level + 1, count_of(level + 1) - 1), level + 1)

    first = ctx * rows
    query_grad, key_grad, value_grad = unit(1, first, 0, False)
    acc[1] += query_grad
    pair[0, :, :, :width] = by_owner(key_grad)
    pair[0, :, :, width:] = by_owner(value_grad)
    pass_on(label_of(0, count_of(0) - 1), 0)
    query_grad, key_grad, value_grad = unit(0, first, 0, True)
    acc[0] += query_grad
    pair[0, :, :, :width] += by_owner(key_grad)
    pair[0, :, :, width:] += by_owner(value_grad)
    query_grad, key_grad, value_grad = unit(1, first, 1, True)
    acc[1] += query_grad
    pair[1, :, :, :width] = by_owner(key_grad)
    pair[1, :, :, width:] = by_owner(value_grad)
    hand_over(0)

    for at in range(2):
        for h in range(heads):
            turned = (acc[at, :, h * run : (h + 1) * run] * scaling).T.astype(jnp.bfloat16)
            dq[h, at * half : (at + 1) * half] = turned.reshape(half, part, width)

    def query_copy(k, block, to):
        return remote(
            dq.at[:, block], dq_out.at[pl.ds(to[1] * heads, heads)], dq_send.at[k], dq_recv.at[k], (to[0], ctx)
        )

    for k in range(1, group):
        query_copy(k, ahead[k], (ahead[k], head)).start()
    stay = pltpu.make_async_copy(dq.at[:, head], dq_out.at[pl.ds(head * heads, heads)], own_sem.at[0])
    stay.start()

    share[...] = combined([0] * levels, -1)[1]
    for j in range(half):
        owner = core * half + j

        @pl.when(owner != head)
        def _():
            remote(
                share.at[j], last.at[chip], end_send.at[j], end_recv.at[chip], (owner, ctx)
            ).start()

        @pl.when(owner == head)
        def _():
            last[chip] = share[j]

    my_half = lax.div(head, half)
    for i in range(half):
        source = i * 2 + my_half

        @pl.when(source != head)
        def _():
            remote(
                share.at[0], last.at[i], end_send.at[0], end_recv.at[i], (source, ctx)
            ).wait_recv()

    total = last[0]
    for i in range(1, half):
        total = total + last[i]
    sums_out[...] = total

    for k in range(1, group):
        query_copy(k, head, (behind[k], behind[k])).wait_recv()
    stay.wait()
    for k in range(1, group):
        query_copy(k, ahead[k], (ahead[k], head)).wait_send()
    for slot in range(cycle):
        to_sibling(slot).wait_send()
        if slot:
            along(slot, (head, ctx)).wait_send()
    for j in range(half):
        owner = core * half + j

        @pl.when(owner != head)
        def _():
            remote(
                share.at[j], last.at[chip], end_send.at[j], end_recv.at[chip], (owner, ctx)
            ).wait_send()


def backward(group, cycle, late, qd, lse, delta, kv):
    heads, rows, wide = qd.shape
    width = wide // 2
    part = rows // group
    half = group // 2
    whole = pl.BlockSpec(memory_space=pltpu.VMEM)
    dma = pltpu.SemaphoreType.DMA
    low = pltpu.VMEM((cycle, half, part, wide), jnp.bfloat16)
    ends = pltpu.VMEM((half, part, wide), jnp.float32)
    return pl.pallas_call(
        functools.partial(backward_kernel, group, cycle),
        out_shape=(
            jax.ShapeDtypeStruct((heads * group, part, width), jnp.bfloat16),
            jax.ShapeDtypeStruct((part, wide), jnp.float32),
        ),
        in_specs=[whole] * 5,
        out_specs=(whole,) * 2,
        scratch_shapes=[
            pltpu.VMEM((2, width, heads * rows // 2), jnp.float32),
            pltpu.VMEM((2, half, part, wide), jnp.float32),
            pltpu.VMEM((heads, group, part, width), jnp.bfloat16),
            pltpu.VMEM((cycle, half, part, wide), jnp.float32),
            low,
            low,
            low,
            low,
            ends,
            ends,
            dma((1,)),
            dma((group,)),
            dma((group,)),
            dma((cycle,)),
            dma((cycle,)),
            dma((cycle,)),
            dma((cycle,)),
            dma((half,)),
            dma((half,)),
        ],
        compiler_params=pltpu.CompilerParams(
            collective_id=1, has_side_effects=True, vmem_limit_bytes=58 * 1024 * 1024
        ),
    )(late, qd, lse, delta, kv)


def local(queries, key_rows, value_rows, attn_output, grad_output, logsumexp, positions):
    cycle = lax.axis_size("ctx")
    group = lax.axis_size("head")
    width = queries.shape[2]
    part = positions.shape[0]
    rows = part * group
    run = rows // 2
    heads = queries.shape[0] // group
    place = positions[0] // run
    low_run = jnp.where(lax.axis_index("head") < group // 2, place, 2 * cycle - 1 - place)
    qd, stats, kv, runs = gather(
        group,
        cycle,
        queries,
        grad_output,
        attn_output,
        logsumexp,
        key_rows,
        value_rows,
        jnp.full((8, 128), low_run, jnp.int32),
    )
    stats = stats.reshape(2, group // 2, heads, 2, part).transpose(3, 0, 2, 1, 4)
    stats = stats.reshape(2, 2, 1, heads * run)
    runs = runs[:, 0, 0]
    late = (runs > low_run).astype(jnp.float32)
    late = jnp.broadcast_to(late[:, None, None], (cycle, 1, heads * run))
    grad_queries, sums = backward(
        group,
        cycle,
        late,
        qd.reshape(heads, rows, 2 * width),
        stats[0],
        stats[1],
        kv.reshape(cycle * rows, 2 * width),
    )
    return grad_queries, sums[:, :width].astype(jnp.bfloat16), sums[:, width:].astype(jnp.bfloat16)


def solution(mesh):
    return jax.shard_map(
        local,
        mesh=mesh,
        in_specs=(
            P(None, ("ctx", "head"), None),
            P(("ctx", "head"), None),
            P(("ctx", "head"), None),
            P(None, ("ctx", "head"), None),
            P(None, ("ctx", "head"), None),
            P(None, ("ctx", "head")),
            P(("ctx", "head")),
        ),
        out_specs=(
            P(None, ("ctx", "head"), None),
            P(("ctx", "head"), None),
            P(("ctx", "head"), None),
        ),
        check_vma=False,
    )
```
